256 devices in a mesh: frame: 32 (over z, y), tok: 8 (over x, core).
Axes of the slice: x: 4, y: 4, z: 8, core: 2. Of those that a mesh axis runs over, the one named last changes fastest.
Arguments:
- queries: bfloat16 [32, 1024, 256], P('frame', 'tok'), may hold values from -120 to 120
- keys: bfloat16 [32, 1024, 256], P('frame', 'tok'), may hold values from -4 to 4
- values: bfloat16 [32, 1024, 256], P('frame', 'tok'), may hold values from -6 to 6
- band: int32 [32, 32], replicated, may hold values from -1 to 7, as said below
Outputs:
- attended: bfloat16 [32, 1024, 256], P('frame', 'tok')
The draws below stay inside these ranges and needn't reach their ends.
Inputs may be any that keep to these rules, and one draw needn't show every extreme that they name: band[i, i] = 7; for |i - j| = 1 the value is 4 or more; for |i - j| >= 2 it is -1 or 0.
All inputs are finite; a program needn't handle non-finite values.
Results may differ from the reference program's by a relative error of at most 0.012.
Values may be sent and summed in bfloat16 or wider, within the bound.
A program may use at most 64 MiB of HBM per device.

```python
import jax
import jax.numpy as jnp
from jax import lax

HD = 128
HEADS = 2
BLOCKS = 8
FRAME_TOK = 1024
FRAMES = 32


def base_normal(key):
    return jnp.clip(jax.random.normal(key, (FRAMES, FRAME_TOK, HEADS * HD), jnp.float32), -4.0, 4.0)


def draw_keys(key, part):
    shared = base_normal(key)
    return shared.astype(jnp.bfloat16)


def draw_queries(key, part):
    key = jax.random.fold_in(key, 23)
    fresh = jnp.clip(jax.random.normal(key, (FRAMES, FRAME_TOK, HEADS * HD), jnp.float32), -4.0, 4.0)
    return fresh.astype(jnp.bfloat16)


def draw_band(key, part):
    key = jax.random.fold_in(key, 7)
    first, second = jax.random.split(key)
    rows_idx = jnp.arange(FRAMES, dtype=jnp.int32)[:, None]
    cols_idx = jnp.arange(FRAMES, dtype=jnp.int32)[None, :]
    distance = jnp.abs(rows_idx - cols_idx)
    level = jnp.zeros((FRAMES, FRAMES), jnp.int32)
    for power in range(1, 14):
        level = level + (distance >= 2 ** power).astype(jnp.int32)
    near_width = BLOCKS - 1 - jax.random.randint(first, (FRAMES, FRAMES), 0, max(BLOCKS // 2, 1))
    chance = jax.random.randint(second, (FRAMES, FRAMES), 0, 1 << 20) % (level + 1)
    far_width = jnp.where(chance == 0, 0, -1)
    band = jnp.where(distance == 0, BLOCKS - 1, jnp.where(distance == 1, near_width, far_width))
    return band.astype(jnp.int32)


def shard_levels(key, shape, pieces, least, high):
    level = 1.0
    for dim, parts in pieces:
        steps = jax.random.uniform(jax.random.fold_in(jax.random.fold_in(key, 6), dim), (parts,), jnp.float32, least / len(pieces), high / len(pieces))
        level = level * jnp.repeat(jnp.exp(steps), shape[dim] // parts).reshape((-1,) + (1,) * (len(shape) - 1 - dim))
    return level


def noise(key, dims, spread, bound, pieces=(), kind=jnp.bfloat16):
    array = jax.random.normal(key, dims, jnp.float32) * spread
    if len(pieces) > 0:
        array = shard_levels(key, dims, pieces, -0.22, 0.18) * array
    return jnp.clip(array, min=-bound, max=bound).astype(kind)


def setup_inputs(seed: int = 0) -> dict:
    key_list = jax.random.split(jax.random.key(seed), 5)
    queries = draw_queries(jax.random.fold_in(key_list[4], 71), 0)
    keys = draw_keys(jax.random.fold_in(key_list[4], 71), 0)
    values = noise(key_list[2], (FRAMES, FRAME_TOK, HEADS * HD), 1.0, 6.0, ((0, 32), (1, 8)))
    band = draw_band(jax.random.fold_in(key_list[4], 71), 0)
    return {"queries": queries, "keys": keys, "values": values, "band": band}


def reference(queries, keys, values, band):
    frames, frame_tok, width = queries.shape
    blocks = BLOCKS
    rows = frame_tok // blocks
    heads = HEADS
    depth = width // heads
    scale = depth ** -0.5
    shape_five = (frames, blocks, rows, heads, depth)
    q_five = queries.reshape(shape_five)
    k_five = keys.reshape(shape_five)
    v_five = values.reshape(shape_five)
    padding = ((1, 1), (0, 0), (0, 0), (0, 0), (0, 0))
    k_padded = jnp.pad(k_five, padding)
    v_padded = jnp.pad(v_five, padding)
    block_ids = jnp.arange(blocks, dtype=jnp.int32)
    frame_ids = jnp.arange(frames, dtype=jnp.int32)

    def one_group(group):
        here = group // blocks
        block = group % blocks
        q_block = lax.dynamic_index_in_dim(lax.dynamic_index_in_dim(q_five, here, 0, False), block, 0, False)
        zero = jnp.zeros((), jnp.int32)
        start = (here, zero, zero, zero, zero)
        size = (3, blocks, rows, heads, depth)
        k_near = lax.dynamic_slice(k_padded, start, size).reshape(3 * blocks * rows, heads, depth)
        v_near = lax.dynamic_slice(v_padded, start, size).reshape(3 * blocks * rows, heads, depth)
        other = here - 1 + jnp.arange(3, dtype=jnp.int32)
        inside = (other >= 0) & (other < frames)
        widths = band[here, jnp.clip(other, 0, frames - 1)]
        near_mask = inside[:, None] & (jnp.abs(block - block_ids)[None, :] <= widths[:, None])
        near_mask = jnp.broadcast_to(near_mask[:, :, None], (3, blocks, rows)).reshape(-1)
        k_far = lax.dynamic_index_in_dim(k_five, block, 1, False).reshape(frames * rows, heads, depth)
        v_far = lax.dynamic_index_in_dim(v_five, block, 1, False).reshape(frames * rows, heads, depth)
        far_keep = (jnp.abs(frame_ids - here) >= 2) & (band[here] >= 0)
        far_mask = jnp.repeat(far_keep, rows)
        k_all = jnp.concatenate([k_near, k_far], axis=0)
        v_all = jnp.concatenate([v_near, v_far], axis=0)
        mask = jnp.concatenate([near_mask, far_mask], axis=0)
        scores = jnp.einsum("qhd,khd->hqk", q_block.astype(jnp.float32), k_all.astype(jnp.float32)) * scale
        scores = jnp.where(mask[None, None, :], scores, -1.0e30)
        top = jnp.max(scores, axis=2)
        weights = jnp.exp(scores - top[:, :, None])
        total = jnp.sum(weights, axis=2)
        result = jnp.einsum("hqk,khd->qhd", weights.astype(jnp.bfloat16).astype(jnp.float32), v_all.astype(jnp.float32))
        result = result / jnp.transpose(total)[:, :, None]
        return result.astype(jnp.bfloat16)

    output = lax.map(one_group, jnp.arange(frames * blocks, dtype=jnp.int32))
    return output.reshape(frames, frame_tok, width)
```

```python
import functools
import math

import jax
import jax.numpy as jnp
from jax import lax
from jax.experimental import pallas as pl
from jax.experimental.pallas import tpu as pltpu
from jax.sharding import PartitionSpec as P

HEADS = 2
HD = 128
ROWS = 128
ZN, YN, XN, CN = 8, 4, 4, 2
FRAMES = ZN * YN
FAR, NEAR = 0, 1
HIDE = -1e30
LOW = -1e29
EXP2_SCALE = HD ** -0.5 * math.log2(math.e)


def coords():
    frame = lax.axis_index("frame")
    tok = lax.axis_index("tok")
    return lax.div(frame, YN), lax.rem(frame, YN), lax.div(tok, CN), lax.rem(tok, CN)


def kernel(
    q_ref, k_ref, v_ref, band_ref, o_ref,
    kvz, kvn, q_own, q_set, bias, acc, top, total,
    o_send, st_send, o_recv, st_recv,
    z_ss, z_rs, n_ss, n_rs, q_ss, q_rs, o_ss, o_rs, s_ss, s_rs,
):
    z, y, x, c = coords()

    def at(dz=0, dy=0, dx=0, dc=0):
        frame = lax.rem(z + (dz + ZN), ZN) * YN + lax.rem(y + (dy + YN), YN)
        tok = lax.rem(x + (dx + XN), XN) * CN + lax.rem(c + dc, CN)
        return (frame, tok)

    def remote(src, dst, ss, rs, to):
        return pltpu.make_async_remote_copy(
            src_ref=src, dst_ref=dst, send_sem=ss, recv_sem=rs,
            device_id=to, device_id_type=pl.DeviceIdType.MESH,
        )

    started = []

    def go(copy):
        copy.start()
        started.append(copy)

    def z_copy(slot, h, src_slot, dz):
        return remote(kvz.at[src_slot, h], kvz.at[slot, h], z_ss.at[slot, h], z_rs.at[slot, h], at(dz=dz))

    def n_copy(slot, src, **to):
        return remote(src, kvn.at[slot], n_ss.at[slot], n_rs.at[slot], at(**to))

    def q_copy(part, k, n):
        to = at(dy=k) if part == FAR else at(dx=k)
        return remote(q_own, q_set.at[part, n - k - 1], q_ss.at[part, n - k - 1], q_rs.at[part, n - k - 1], to)

    def o_copies(part, k, n, h):
        to = at(dy=k) if part == FAR else at(dx=k)
        there = n - k - 1
        return (
            remote(o_send.at[part, k - 1, h], o_recv.at[part, there, h], o_ss.at[part, there, h], o_rs.at[part, there, h], to),
            remote(st_send.at[part, k - 1, h], st_recv.at[part, there, h], s_ss.at[part, there, h], s_rs.at[part, there, h], to),
        )

    barrier = pltpu.get_barrier_semaphore()
    peers = [at(dz=1), at(dz=-1), at(dz=2), at(dz=-2), at(dy=1), at(dy=2), at(dy=3), at(dx=1), at(dx=2), at(dx=3), at(dc=1)]
    for peer in peers:
        pl.semaphore_signal(barrier, inc=1, device_id=peer, device_id_type=pl.DeviceIdType.MESH)

    for h in range(HEADS):
        cols = slice(h * HD, (h + 1) * HD)
        kvz[0, h, 0:ROWS] = k_ref[:, cols]
        kvz[0, h, ROWS:2 * ROWS] = v_ref[:, cols].T
        q_own[h] = q_ref[:, cols].T

    lane = lax.broadcasted_iota(jnp.int32, (1, 4 * ROWS), 1) // ROWS

    def row_of(cells):
        row = jnp.full((1, 4 * ROWS), cells[0], jnp.float32)
        for k in range(1, 4):
            row = jnp.where(lane == k, cells[k], row)
        return row

    frame = z * YN + y
    for slot in range(ZN):
        key_frame = lax.rem(z + (ZN - slot), ZN) * YN + y
        cells = []
        for k in range(YN):
            query_frame = z * YN + lax.rem(y + k, YN)
            seen = (jnp.abs(query_frame - key_frame) >= 2) & (band_ref[query_frame, key_frame] >= 0)
            cells.append(jnp.where(seen, 0.0, HIDE).astype(jnp.float32))
        bias[slot] = row_of(cells)
    for step in range(3):
        key_frame = frame + (step - 1)
        inside = (key_frame >= 0) & (key_frame < FRAMES)
        reach = band_ref[frame, jnp.clip(key_frame, 0, FRAMES - 1)]
        for other in range(CN):
            key_block = x * CN + lax.rem(c + other, CN)
            cells = []
            for k in range(XN):
                query_block = lax.rem(x + k, XN) * CN + c
                seen = inside & (jnp.abs(query_block - key_block) <= reach)
                cells.append(jnp.where(seen, 0.0, HIDE).astype(jnp.float32))
            bias[ZN + step * CN + other] = row_of(cells)

    pl.semaphore_wait(barrier, len(peers))

    for h in range(HEADS):
        go(z_copy(1, h, 0, 1))
        go(z_copy(7, h, 0, -1))
    for k in (2, 1, 3):
        go(q_copy(FAR, k, YN))
        go(q_copy(NEAR, k, XN))
    go(n_copy(0, kvz.at[0], dc=1))
    before = n_copy(1, kvz.at[0], dy=1)
    after = n_copy(3, kvz.at[0], dy=-1)
    started.extend([before, after])

    @pl.when(y < YN - 1)
    def _():
        before.start()

    @pl.when(y > 0)
    def _():
        after.start()

    def update(part, h, blocks, first):
        heads = [q_own[h]] + [q_set[part, k, h] for k in range(3)]
        qt = jnp.concatenate(heads, axis=1)
        rows = [bias[b] for _, b in blocks]
        scores = [jnp.dot(ref[0:ROWS], qt, preferred_element_type=jnp.float32) for ref, _ in blocks]
        high = functools.reduce(jnp.maximum, [jnp.max(s, axis=0, keepdims=True) + r for s, r in zip(scores, rows)])
        old = jnp.full((1, 4 * ROWS), LOW, jnp.float32) if first else top[part, h]
        new = jnp.maximum(old, high)
        weights = [jnp.exp2((s - (new - r)) * EXP2_SCALE) for s, r in zip(scores, rows)]
        add = functools.reduce(jnp.add, [jnp.sum(w, axis=0, keepdims=True) for w in weights])
        wt = jnp.concatenate([w.astype(jnp.bfloat16) for w in weights], axis=0)
        vt = jnp.concatenate([ref[ROWS:2 * ROWS] for ref, _ in blocks], axis=1)
        out = jnp.dot(vt, wt, preferred_element_type=jnp.float32)
        top[part, h] = new
        if first:
            total[part, h] = add
            acc[part, h] = out
        else:
            factor = jnp.exp2((old - new) * EXP2_SCALE)
            total[part, h] = total[part, h] * factor + add
            acc[part, h] = acc[part, h] * factor + out

    def far(h, slots, first=False):
        update(FAR, h, [(kvz.at[s, h], s) for s in slots], first)

    def near(h, refs, first=False):
        update(NEAR, h, [(ref.at[h], b) for ref, b in refs], first)

    def send_out(part, h, n):
        for k in (2, 1, 3):
            cols = slice(k * ROWS, (k + 1) * ROWS)
            o_send[part, k - 1, h] = acc[part, h, :, cols].astype(jnp.bfloat16)
            st_send[part, k - 1, h] = jnp.concatenate(
                [top[part, h, :, cols], total[part, h, :, cols], jnp.zeros((6, ROWS), jnp.float32)], axis=0
            )
            for copy in o_copies(part, k, n, h):
                go(copy)

    def z_wait(slot, h):
        z_copy(slot, h, 0, 1).wait_recv()

    for h in range(HEADS):
        z_wait(1, h)
        go(z_copy(2, h, 1, 1))
        z_wait(7, h)
        go(z_copy(6, h, 7, -1))

    @pl.when(y == YN - 1)
    def _():
        n_copy(1, kvz.at[1], dy=1).start()

    @pl.when(y == 0)
    def _():
        n_copy(3, kvz.at[7], dy=-1).start()

    n_copy(0, kvz.at[0], dc=1).wait_recv()
    for k in range(1, XN):
        q_copy(NEAR, k, XN).wait_recv()
    for h in range(HEADS):
        near(h, [(kvz.at[0], ZN + 2), (kvn.at[0], ZN + 3)], first=True)
    for k in range(1, YN):
        q_copy(FAR, k, YN).wait_recv()
    for h in range(HEADS):
        far(h, (0, 1, 7), first=True)

    for slot in (1, 3):
        n_copy(slot, kvz.at[0], dy=1).wait_recv()
        go(n_copy(slot + 1, kvn.at[slot], dc=1))

    for h in range(HEADS):
        z_wait(2, h)
        if h == 0:
            go(z_copy(4, h, 2, 2))
        go(z_copy(3, h, 2, 1))
        z_wait(6, h)
        if h == 1:
            go(z_copy(4, h, 6, -2))
        go(z_copy(5, h, 6, -1))

    for slot in (2, 4):
        n_copy(slot, kvz.at[0], dc=1).wait_recv()
    for h in range(HEADS):
        near(h, [(kvn.at[1], ZN), (kvn.at[2], ZN + 1)])
        near(h, [(kvn.at[3], ZN + 4), (kvn.at[4], ZN + 5)])
        send_out(NEAR, h, XN)
    for h in range(HEADS):
        far(h, (2, 6))
    for h in range(HEADS):
        z_wait(3, h)
        z_wait(5, h)
        far(h, (3, 5))
    for h in range(HEADS):
        z_wait(4, h)
        far(h, (4,))
        send_out(FAR, h, YN)

    def merged(h, state, parts):
        for part in parts:
            for k in range(3):
                for copy in o_copies(part, k + 1, 4, h):
                    copy.wait_recv()
        high, count, out = state
        tops = [high] + [st_recv[part, k, h, 0:1] for part in parts for k in range(3)]
        counts = [count] + [st_recv[part, k, h, 1:2] for part in parts for k in range(3)]
        outs = [out] + [o_recv[part, k, h].astype(jnp.float32) for part in parts for k in range(3)]
        new = functools.reduce(jnp.maximum, tops)
        factors = [jnp.exp2((t - new) * EXP2_SCALE) for t in tops]
        count = functools.reduce(jnp.add, [n * f for n, f in zip(counts, factors)])
        out = functools.reduce(jnp.add, [o * f for o, f in zip(outs, factors)])
        return new, count, out

    own = slice(0, ROWS)
    states = []
    for h in range(HEADS):
        one = (top[NEAR, h, :, own], total[NEAR, h, :, own], acc[NEAR, h, :, own])
        two = (top[FAR, h, :, own], total[FAR, h, :, own], acc[FAR, h, :, own])
        new = jnp.maximum(one[0], two[0])
        f1 = jnp.exp2((one[0] - new) * EXP2_SCALE)
        f2 = jnp.exp2((two[0] - new) * EXP2_SCALE)
        states.append(merged(h, (new, one[1] * f1 + two[1] * f2, one[2] * f1 + two[2] * f2), (NEAR,)))
    for h in range(HEADS):
        _, count, out = merged(h, states[h], (FAR,))
        o_ref[:, h * HD:(h + 1) * HD] = (out / count).T.astype(jnp.bfloat16)
    for copy in started:
        copy.wait_send()


def shards(queries, keys, values, band):
    vmem = pl.BlockSpec(memory_space=pltpu.VMEM)
    bf16, f32 = jnp.bfloat16, jnp.float32
    dma = pltpu.SemaphoreType.DMA
    out = pl.pallas_call(
        kernel,
        out_shape=jax.ShapeDtypeStruct((ROWS, HEADS * HD), bf16),
        in_specs=[vmem, vmem, vmem, pl.BlockSpec(memory_space=pltpu.SMEM)],
        out_specs=vmem,
        scratch_shapes=[
            pltpu.VMEM((ZN, HEADS, 2 * ROWS, HD), bf16),
            pltpu.VMEM((5, HEADS, 2 * ROWS, HD), bf16),
            pltpu.VMEM((HEADS, HD, ROWS), bf16),
            pltpu.VMEM((2, 3, HEADS, HD, ROWS), bf16),
            pltpu.VMEM((ZN + 6, 1, 4 * ROWS), f32),
            pltpu.VMEM((2, HEADS, HD, 4 * ROWS), f32),
            pltpu.VMEM((2, HEADS, 1, 4 * ROWS), f32),
            pltpu.VMEM((2, HEADS, 1, 4 * ROWS), f32),
            pltpu.VMEM((2, 3, HEADS, HD, ROWS), bf16),
            pltpu.VMEM((2, 3, HEADS, 8, ROWS), f32),
            pltpu.VMEM((2, 3, HEADS, HD, ROWS), bf16),
            pltpu.VMEM((2, 3, HEADS, 8, ROWS), f32),
            dma((ZN, HEADS)), dma((ZN, HEADS)),
            dma((5,)), dma((5,)),
            dma((2, 3)), dma((2, 3)),
            dma((2, 3, HEADS)), dma((2, 3, HEADS)),
            dma((2, 3, HEADS)), dma((2, 3, HEADS)),
        ],
        compiler_params=pltpu.CompilerParams(collective_id=0, has_side_effects=True, vmem_limit_bytes=32 * 2 ** 20),
    )(queries[0], keys[0], values[0], band)
    return out[None]


def solution(mesh):
    spec = P("frame", "tok", None)
    return jax.shard_map(shards, mesh=mesh, in_specs=(spec, spec, spec, P()), out_specs=spec, check_vma=False)
```

```python
import functools
import math

import jax
import jax.numpy as jnp
from jax import lax
from jax.experimental import pallas as pl
from jax.experimental.pallas import tpu as pltpu
from jax.sharding import PartitionSpec as P

HEADS = 2
HD = 128
ROWS = 128
ZN, YN, XN, CN = 8, 4, 4, 2
FRAMES = ZN * YN
FAR, NEAR = 0, 1
K, V = 0, 1
HIDE = -1e30
LOW = -1e29
EXP2_SCALE = HD ** -0.5 * math.log2(math.e)


def coords():
    frame = lax.axis_index("frame")
    tok = lax.axis_index("tok")
    return lax.div(frame, YN), lax.rem(frame, YN), lax.div(tok, CN), lax.rem(tok, CN)


def kernel(
    q_ref, k_ref, v_ref, band_ref, o_ref,
    v_in, q_in, band_in, kz, vz, kn, vn, q_own, q_set, bias, acc, top, total,
    o_send, st_send, o_recv, st_recv,
    in_sem, z_ss, z_rs, n_ss, n_rs, q_ss, q_rs, o_ss, o_rs, s_ss, s_rs,
):
    z, y, x, c = coords()

    def at(dz=0, dy=0, dx=0, dc=0):
        frame = lax.rem(z + (dz + ZN), ZN) * YN + lax.rem(y + (dy + YN), YN)
        tok = lax.rem(x + (dx + XN), XN) * CN + lax.rem(c + dc, CN)
        return (frame, tok)

    def remote(src, dst, ss, rs, to):
        return pltpu.make_async_remote_copy(
            src_ref=src, dst_ref=dst, send_sem=ss, recv_sem=rs,
            device_id=to, device_id_type=pl.DeviceIdType.MESH,
        )

    barrier = pltpu.get_barrier_semaphore()
    peers = [at(dz=1), at(dz=-1), at(dz=2), at(dz=-2), at(dy=1), at(dy=2), at(dy=3), at(dx=1), at(dx=2), at(dx=3), at(dc=1)]
    for peer in peers:
        pl.semaphore_signal(barrier, inc=1, device_id=peer, device_id_type=pl.DeviceIdType.MESH)

    loads = [
        pltpu.make_async_copy(src, dst, in_sem.at[i])
        for i, (src, dst) in enumerate(((v_ref, v_in), (k_ref, kz.at[0]), (q_ref, q_in), (band_ref, band_in)))
    ]
    for load in loads:
        load.start()

    started = []

    def go(copy):
        copy.start()
        started.append(copy)

    def piece(keys, values, h, kind):
        part = pl.ds(h * HD, HD)
        return keys.at[:, part] if kind == K else values.at[part]

    def z_copy(slot, h, kind, src, dz):
        return remote(
            piece(kz.at[src], vz.at[src], h, kind), piece(kz.at[slot], vz.at[slot], h, kind),
            z_ss.at[slot, h, kind], z_rs.at[slot, h, kind], at(dz=dz),
        )

    def z_wait(slot, h, kind):
        z_copy(slot, h, kind, 0, 1).wait_recv()

    def n_copy(slot, h, kind, keys, values, **to):
        return remote(
            piece(keys, values, h, kind), piece(kn.at[slot], vn.at[slot], h, kind),
            n_ss.at[slot, h, kind], n_rs.at[slot, h, kind], at(**to),
        )

    def n_wait(slot, h, kind):
        n_copy(slot, h, kind, kz.at[0], vz.at[0], dc=1).wait_recv()

    def q_copy(part, k, n):
        to = at(dy=k) if part == FAR else at(dx=k)
        return remote(q_own, q_set.at[part, n - k - 1], q_ss.at[part, n - k - 1], q_rs.at[part, n - k - 1], to)

    def o_copies(part, k, n, h):
        to = at(dy=k) if part == FAR else at(dx=k)
        there = n - k - 1
        return (
            remote(o_send.at[part, k - 1, h], o_recv.at[part, there, h], o_ss.at[part, there, h], o_rs.at[part, there, h], to),
            remote(st_send.at[part, k - 1, h], st_recv.at[part, there, h], s_ss.at[part, there, h], s_rs.at[part, there, h], to),
        )

    loads[0].wait()
    vz[0] = v_in[...].T
    loads[1].wait()
    pl.semaphore_wait(barrier, len(peers))

    for kind in (K, V):
        for h in range(HEADS):
            go(z_copy(1, h, kind, 0, 1))
            go(z_copy(7, h, kind, 0, -1))

    loads[2].wait()
    q_own[...] = q_in[...].T
    for k in (2, 1, 3):
        go(q_copy(NEAR, k, XN))
        go(q_copy(FAR, k, YN))
    pieces = [(h, kind) for h in range(HEADS) for kind in (K, V)]
    before = [n_copy(1, h, kind, kz.at[0], vz.at[0], dy=1) for h, kind in pieces]
    after = [n_copy(3, h, kind, kz.at[0], vz.at[0], dy=-1) for h, kind in pieces]
    started.extend(before + after)

    @pl.when(y < YN - 1)
    def _():
        for copy in before:
            copy.start()

    @pl.when(y > 0)
    def _():
        for copy in after:
            copy.start()

    for h, kind in pieces:
        go(n_copy(0, h, kind, kz.at[0], vz.at[0], dc=1))

    loads[3].wait()
    lane = lax.broadcasted_iota(jnp.int32, (1, 4 * ROWS), 1) // ROWS

    def row_of(cells):
        row = jnp.full((1, 4 * ROWS), cells[0], jnp.float32)
        for k in range(1, 4):
            row = jnp.where(lane == k, cells[k], row)
        return row

    frame = z * YN + y
    for slot in range(ZN):
        key_frame = lax.rem(z + (ZN - slot), ZN) * YN + y
        cells = []
        for k in range(YN):
            query_frame = z * YN + lax.rem(y + k, YN)
            seen = (jnp.abs(query_frame - key_frame) >= 2) & (band_in[query_frame, key_frame] >= 0)
            cells.append(jnp.where(seen, 0.0, HIDE).astype(jnp.float32))
        bias[slot] = row_of(cells)
    for step in range(3):
        key_frame = frame + (step - 1)
        inside = (key_frame >= 0) & (key_frame < FRAMES)
        reach = band_in[frame, jnp.clip(key_frame, 0, FRAMES - 1)]
        for other in range(CN):
            key_block = x * CN + lax.rem(c + other, CN)
            cells = []
            for k in range(XN):
                query_block = lax.rem(x + k, XN) * CN + c
                seen = inside & (jnp.abs(query_block - key_block) <= reach)
                cells.append(jnp.where(seen, 0.0, HIDE).astype(jnp.float32))
            bias[ZN + step * CN + other] = row_of(cells)

    def update(part, h, blocks, first):
        cols = pl.ds(h * HD, HD)
        qt = jnp.concatenate([q_own[cols]] + [q_set[part, k, cols] for k in range(3)], axis=1)
        rows = [bias[b] for _, _, b in blocks]
        scores = [jnp.dot(keys[:, cols], qt, preferred_element_type=jnp.float32) for keys, _, _ in blocks]
        high = functools.reduce(jnp.maximum, [jnp.max(s, axis=0, keepdims=True) + r for s, r in zip(scores, rows)])
        old = jnp.full((1, 4 * ROWS), LOW, jnp.float32) if first else top[part, h]
        new = jnp.maximum(old, high)
        weights = [jnp.exp2((s - (new - r)) * EXP2_SCALE) for s, r in zip(scores, rows)]
        add = functools.reduce(jnp.add, [jnp.sum(w, axis=0, keepdims=True) for w in weights])
        wt = jnp.concatenate([w.astype(jnp.bfloat16) for w in weights], axis=0)
        vt = jnp.concatenate([values[cols] for _, values, _ in blocks], axis=1)
        out = jnp.dot(vt, wt, preferred_element_type=jnp.float32)
        top[part, h] = new
        if first:
            total[part, h] = add
            acc[part, h] = out
        else:
            factor = jnp.exp2((old - new) * EXP2_SCALE)
            total[part, h] = total[part, h] * factor + add
            acc[part, h] = acc[part, h] * factor + out

    def far(h, slots, first=False):
        update(FAR, h, [(kz.at[s], vz.at[s], s) for s in slots], first)

    def near(h, refs, first=False):
        update(NEAR, h, [(keys, values, b) for keys, values, b in refs], first)

    def send_out(part, h, n):
        for k in (2, 1, 3):
            cols = slice(k * ROWS, (k + 1) * ROWS)
            o_send[part, k - 1, h] = acc[part, h, :, cols].astype(jnp.bfloat16)
            st_send[part, k - 1, h] = jnp.concatenate(
                [top[part, h, :, cols], total[part, h, :, cols], jnp.zeros((6, ROWS), jnp.float32)], axis=0
            )
            for copy in o_copies(part, k, n, h):
                go(copy)

    for kind in (K, V):
        for h in range(HEADS):
            z_wait(1, h, kind)
            go(z_copy(2, h, kind, 1, 1))

            @pl.when(y == YN - 1)
            def _(h=h, kind=kind):
                n_copy(1, h, kind, kz.at[1], vz.at[1], dy=1).start()

            z_wait(7, h, kind)
            go(z_copy(6, h, kind, 7, -1))

            @pl.when(y == 0)
            def _(h=h, kind=kind):
                n_copy(3, h, kind, kz.at[7], vz.at[7], dy=-1).start()

    for h, kind in pieces:
        n_wait(0, h, kind)
    for k in range(1, XN):
        q_copy(NEAR, k, XN).wait_recv()
    for h in range(HEADS):
        near(h, [(kz.at[0], vz.at[0], ZN + 2), (kn.at[0], vn.at[0], ZN + 3)], first=True)
    for k in range(1, YN):
        q_copy(FAR, k, YN).wait_recv()
    far(0, (0, 1, 7), first=True)

    for h in range(HEADS):
        for kind in (K, V):
            z_wait(2, h, kind)
            go(z_copy(3, h, kind, 2, 1))
            if kind == K:
                go(z_copy(4, h, kind, 2, 2))
            z_wait(6, h, kind)
            go(z_copy(5, h, kind, 6, -1))
            if kind == V:
                go(z_copy(4, h, kind, 6, -2))

    for h, kind in pieces:
        for slot in (1, 3):
            n_wait(slot, h, kind)
            go(n_copy(slot + 1, h, kind, kn.at[slot], vn.at[slot], dc=1))
    far(1, (0, 1, 7), first=True)
    for h in range(HEADS):
        far(h, (2, 6))
    for h in range(HEADS):
        for slot in (2, 4):
            for kind in (K, V):
                n_wait(slot, h, kind)
        near(h, [(kn.at[1], vn.at[1], ZN), (kn.at[2], vn.at[2], ZN + 1)])
        near(h, [(kn.at[3], vn.at[3], ZN + 4), (kn.at[4], vn.at[4], ZN + 5)])
        send_out(NEAR, h, XN)
    for h in range(HEADS):
        for slot in (3, 5, 4):
            for kind in (K, V):
                z_wait(slot, h, kind)
        far(h, (4, 3, 5))
        send_out(FAR, h, YN)

    def merged(h, state, part):
        for k in range(3):
            for copy in o_copies(part, k + 1, 4, h):
                copy.wait_recv()
        high, count, out = state
        tops = [high] + [st_recv[part, k, h, 0:1] for k in range(3)]
        counts = [count] + [st_recv[part, k, h, 1:2] for k in range(3)]
        outs = [out] + [o_recv[part, k, h].astype(jnp.float32) for k in range(3)]
        new = functools.reduce(jnp.maximum, tops)
        factors = [jnp.exp2((t - new) * EXP2_SCALE) for t in tops]
        count = functools.reduce(jnp.add, [n * f for n, f in zip(counts, factors)])
        out = functools.reduce(jnp.add, [o * f for o, f in zip(outs, factors)])
        return new, count, out

    own = slice(0, ROWS)
    states = []
    for h in range(HEADS):
        one = (top[NEAR, h, :, own], total[NEAR, h, :, own], acc[NEAR, h, :, own])
        two = (top[FAR, h, :, own], total[FAR, h, :, own], acc[FAR, h, :, own])
        new = jnp.maximum(one[0], two[0])
        f1 = jnp.exp2((one[0] - new) * EXP2_SCALE)
        f2 = jnp.exp2((two[0] - new) * EXP2_SCALE)
        states.append(merged(h, (new, one[1] * f1 + two[1] * f2, one[2] * f1 + two[2] * f2), NEAR))
    for h in range(HEADS):
        _, count, out = merged(h, states[h], FAR)
        o_ref[:, h * HD:(h + 1) * HD] = (out / count).T.astype(jnp.bfloat16)
    for copy in started:
        copy.wait_send()


def shards(queries, keys, values, band):
    vmem = pl.BlockSpec(memory_space=pltpu.VMEM)
    bf16, f32 = jnp.bfloat16, jnp.float32
    dma = pltpu.SemaphoreType.DMA
    width = HEADS * HD
    out = pl.pallas_call(
        kernel,
        out_shape=jax.ShapeDtypeStruct((ROWS, width), bf16),
        in_specs=[pl.BlockSpec(memory_space=pltpu.HBM)] * 4,
        out_specs=vmem,
        scratch_shapes=[
            pltpu.VMEM((ROWS, width), bf16),
            pltpu.VMEM((ROWS, width), bf16),
            pltpu.SMEM((FRAMES, FRAMES), jnp.int32),
            pltpu.VMEM((ZN, ROWS, width), bf16),
            pltpu.VMEM((ZN, width, ROWS), bf16),
            pltpu.VMEM((5, ROWS, width), bf16),
            pltpu.VMEM((5, width, ROWS), bf16),
            pltpu.VMEM((width, ROWS), bf16),
            pltpu.VMEM((2, 3, width, ROWS), bf16),
            pltpu.VMEM((ZN + 6, 1, 4 * ROWS), f32),
            pltpu.VMEM((2, HEADS, HD, 4 * ROWS), f32),
            pltpu.VMEM((2, HEADS, 1, 4 * ROWS), f32),
            pltpu.VMEM((2, HEADS, 1, 4 * ROWS), f32),
            pltpu.VMEM((2, 3, HEADS, HD, ROWS), bf16),
            pltpu.VMEM((2, 3, HEADS, 8, ROWS), f32),
            pltpu.VMEM((2, 3, HEADS, HD, ROWS), bf16),
            pltpu.VMEM((2, 3, HEADS, 8, ROWS), f32),
            dma((4,)),
            dma((ZN, HEADS, 2)), dma((ZN, HEADS, 2)),
            dma((5, HEADS, 2)), dma((5, HEADS, 2)),
            dma((2, 3)), dma((2, 3)),
            dma((2, 3, HEADS)), dma((2, 3, HEADS)),
            dma((2, 3, HEADS)), dma((2, 3, HEADS)),
        ],
        compiler_params=pltpu.CompilerParams(collective_id=0, has_side_effects=True, vmem_limit_bytes=55100 * 2 ** 10),
    )(queries[0], keys[0], values[0], band)
    return out[None]


def solution(mesh):
    spec = P("frame", "tok", None)
    return jax.shard_map(shards, mesh=mesh, in_specs=(spec, spec, spec, P()), out_specs=spec, check_vma=False)
```

```python
import functools
import math

import jax
import jax.numpy as jnp
from jax import lax
from jax.experimental import pallas as pl
from jax.experimental.pallas import tpu as pltpu
from jax.sharding import PartitionSpec as P

HEADS = 2
HD = 128
ROWS = 128
ZN, YN, XN, CN = 8, 4, 4, 2
FRAMES = ZN * YN
FAR, NEAR = 0, 1
K, V = 0, 1
HIDE = -1e30
LOW = -1e29
EXP2_SCALE = HD ** -0.5 * math.log2(math.e)


def coords():
    frame = lax.axis_index("frame")
    tok = lax.axis_index("tok")
    return lax.div(frame, YN), lax.rem(frame, YN), lax.div(tok, CN), lax.rem(tok, CN)


def kernel(
    q_ref, k_ref, v_ref, band_ref, o_ref,
    v_in, q_in, band_in, kz, vz, kn, vn, q_own, q_set, bias, acc, top, total,
    o_send, st_send, o_recv, st_recv,
    in_sem, z_ss, z_rs, n_ss, n_rs, q_ss, q_rs, o_ss, o_rs, s_ss, s_rs,
):
    z, y, x, c = coords()

    def at(dz=0, dy=0, dx=0, dc=0):
        frame = lax.rem(z + (dz + ZN), ZN) * YN + lax.rem(y + (dy + YN), YN)
        tok = lax.rem(x + (dx + XN), XN) * CN + lax.rem(c + dc, CN)
        return (frame, tok)

    def remote(src, dst, ss, rs, to):
        return pltpu.make_async_remote_copy(
            src_ref=src, dst_ref=dst, send_sem=ss, recv_sem=rs,
            device_id=to, device_id_type=pl.DeviceIdType.MESH,
        )

    barrier = pltpu.get_barrier_semaphore()
    peers = [at(dz=1), at(dz=-1), at(dz=2), at(dz=-2), at(dy=1), at(dy=2), at(dy=3), at(dx=1), at(dx=2), at(dx=3), at(dc=1)]
    for peer in peers:
        pl.semaphore_signal(barrier, inc=1, device_id=peer, device_id_type=pl.DeviceIdType.MESH)

    loads = [
        pltpu.make_async_copy(src, dst, in_sem.at[i])
        for i, (src, dst) in enumerate(((v_ref, v_in), (k_ref, kz.at[0]), (q_ref, q_in), (band_ref, band_in)))
    ]
    for load in loads:
        load.start()

    started = []

    def go(copy):
        copy.start()
        started.append(copy)

    def piece(keys, values, h, kind):
        part = pl.ds(h * HD, HD)
        return keys.at[:, part] if kind == K else values.at[part]

    def z_copy(slot, h, kind, src, dz):
        return remote(
            piece(kz.at[src], vz.at[src], h, kind), piece(kz.at[slot], vz.at[slot], h, kind),
            z_ss.at[slot, h, kind], z_rs.at[slot, h, kind], at(dz=dz),
        )

    def z_wait(slot, h, kind):
        z_copy(slot, h, kind, 0, 1).wait_recv()

    def n_copy(slot, h, kind, keys, values, **to):
        return remote(
            piece(keys, values, h, kind), piece(kn.at[slot], vn.at[slot], h, kind),
            n_ss.at[slot, h, kind], n_rs.at[slot, h, kind], at(**to),
        )

    def n_wait(slot, h, kind):
        n_copy(slot, h, kind, kz.at[0], vz.at[0], dc=1).wait_recv()

    def q_copy(part, k, n):
        to = at(dy=k) if part == FAR else at(dx=k)
        return remote(q_own, q_set.at[part, n - k - 1], q_ss.at[part, n - k - 1], q_rs.at[part, n - k - 1], to)

    def o_copies(part, k, n, h):
        to = at(dy=k) if part == FAR else at(dx=k)
        there = n - k - 1
        return (
            remote(o_send.at[part, k - 1, h], o_recv.at[part, there, h], o_ss.at[part, there, h], o_rs.at[part, there, h], to),
            remote(st_send.at[part, k - 1, h], st_recv.at[part, there, h], s_ss.at[part, there, h], s_rs.at[part, there, h], to),
        )

    frame = z * YN + y
    loads[0].wait()
    vz[0] = v_in[...].T
    loads[1].wait()
    pl.semaphore_wait(barrier, len(peers))

    for kind in (K, V):
        for h in range(HEADS):
            go(z_copy(1, h, kind, 0, 1))
            go(z_copy(7, h, kind, 0, -1))

    pieces = [(h, kind) for h in range(HEADS) for kind in (K, V)]
    before = [n_copy(1, h, kind, kz.at[0], vz.at[0], dy=1) for h, kind in pieces]
    after = [n_copy(3, h, kind, kz.at[0], vz.at[0], dy=-1) for h, kind in pieces]

    @pl.when((y < YN - 1))
    def _():
        for copy in before:
            copy.start()

    @pl.when(y > 0)
    def _():
        for copy in after:
            copy.start()

    for h, kind in pieces:
        go(n_copy(0, h, kind, kz.at[0], vz.at[0], dc=1))

    @pl.when(frame == 0)
    def _():
        kn[1:3] = jnp.zeros((2,) + kn.shape[1:], kn.dtype)
        vn[1:3] = jnp.zeros((2,) + vn.shape[1:], vn.dtype)

    @pl.when(frame == FRAMES - 1)
    def _():
        kn[3:5] = jnp.zeros((2,) + kn.shape[1:], kn.dtype)
        vn[3:5] = jnp.zeros((2,) + vn.shape[1:], vn.dtype)

    loads[2].wait()
    q_own[...] = q_in[...].T
    for k in (2, 1, 3):
        go(q_copy(NEAR, k, XN))
        go(q_copy(FAR, k, YN))
    loads[3].wait()
    lane = lax.broadcasted_iota(jnp.int32, (1, 4 * ROWS), 1) // ROWS

    def row_of(cells):
        row = jnp.full((1, 4 * ROWS), cells[0], jnp.float32)
        for k in range(1, 4):
            row = jnp.where(lane == k, cells[k], row)
        return row

    for slot in range(ZN):
        key_frame = lax.rem(z + (ZN - slot), ZN) * YN + y
        cells = []
        for k in range(YN):
            query_frame = z * YN + lax.rem(y + k, YN)
            seen = (jnp.abs(query_frame - key_frame) >= 2) & (band_in[query_frame, key_frame] >= 0)
            cells.append(jnp.where(seen, 0.0, HIDE).astype(jnp.float32))
        bias[slot] = row_of(cells)
    for step in range(3):
        key_frame = frame + (step - 1)
        inside = (key_frame >= 0) & (key_frame < FRAMES)
        reach = band_in[frame, jnp.clip(key_frame, 0, FRAMES - 1)]
        for other in range(CN):
            key_block = x * CN + lax.rem(c + other, CN)
            cells = []
            for k in range(XN):
                query_block = lax.rem(x + k, XN) * CN + c
                seen = inside & (jnp.abs(query_block - key_block) <= reach)
                cells.append(jnp.where(seen, 0.0, HIDE).astype(jnp.float32))
            bias[ZN + step * CN + other] = row_of(cells)

    def update(part, h, blocks, first, before_values=lambda: None):
        cols = pl.ds(h * HD, HD)
        qt = jnp.concatenate([q_own[cols]] + [q_set[part, k, cols] for k in range(3)], axis=1)
        rows = [bias[b] for _, _, b in blocks]
        scores = [jnp.dot(keys[:, cols], qt, preferred_element_type=jnp.float32) for keys, _, _ in blocks]
        high = functools.reduce(jnp.maximum, [jnp.max(s, axis=0, keepdims=True) + r for s, r in zip(scores, rows)])
        old = jnp.full((1, 4 * ROWS), LOW, jnp.float32) if first else top[part, h]
        new = jnp.maximum(old, high)
        weights = [jnp.exp2((s - (new - r)) * EXP2_SCALE) for s, r in zip(scores, rows)]
        add = functools.reduce(jnp.add, [jnp.sum(w, axis=0, keepdims=True) for w in weights])
        top[part, h] = new
        if first:
            total[part, h] = add
        else:
            factor = jnp.exp2((old - new) * EXP2_SCALE)
            total[part, h] = total[part, h] * factor + add
        wt = jnp.concatenate([w.astype(jnp.bfloat16) for w in weights], axis=0)
        before_values()
        vt = jnp.concatenate([values[cols] for _, values, _ in blocks], axis=1)
        out = jnp.dot(vt, wt, preferred_element_type=jnp.float32)
        if first:
            acc[part, h] = out
        else:
            acc[part, h] = acc[part, h] * factor + out

    def far(h, slots, first=False, before_values=lambda: None):
        update(FAR, h, [(kz.at[s], vz.at[s], s) for s in slots], first, before_values)

    def near(h, refs, first=False):
        update(NEAR, h, [(keys, values, b) for keys, values, b in refs], first)

    def send_out(part, h, n):
        for k in (2, 1, 3):
            cols = slice(k * ROWS, (k + 1) * ROWS)
            o_send[part, k - 1, h] = acc[part, h, :, cols].astype(jnp.bfloat16)
            st_send[part, k - 1, h] = jnp.concatenate(
                [top[part, h, :, cols], total[part, h, :, cols], jnp.zeros((6, ROWS), jnp.float32)], axis=0
            )
            for copy in o_copies(part, k, n, h):
                go(copy)

    for kind in (K, V):
        for h in range(HEADS):
            z_wait(1, h, kind)
            go(z_copy(2, h, kind, 1, 1))

            @pl.when((y == YN - 1) & (z > 0))
            def _(h=h, kind=kind):
                n_copy(1, h, kind, kz.at[1], vz.at[1], dy=1).start()

            z_wait(7, h, kind)
            go(z_copy(6, h, kind, 7, -1))

            @pl.when((y == 0) & (z < ZN - 1))
            def _(h=h, kind=kind):
                n_copy(3, h, kind, kz.at[7], vz.at[7], dy=-1).start()

    def hand_over(slot, h):
        for kind in (K, V):
            n_wait(slot, h, kind)
            n_copy(slot + 1, h, kind, kn.at[slot], vn.at[slot], dc=1).start()

    @pl.when(y > 0)
    def _():
        for h in range(HEADS):
            hand_over(1, h)

    @pl.when(y < YN - 1)
    def _():
        for h in range(HEADS):
            hand_over(3, h)

    for h, kind in pieces:
        n_wait(0, h, kind)
    for k in range(1, XN):
        q_copy(NEAR, k, XN).wait_recv()
    for h in range(HEADS):
        near(h, [(kz.at[0], vz.at[0], ZN + 2), (kn.at[0], vn.at[0], ZN + 3)], first=True)

    for h in range(HEADS):
        for kind in (K, V):
            z_wait(2, h, kind)
            go(z_copy(3, h, kind, 2, 1))
            if kind == K:
                go(z_copy(4, h, kind, 2, 2))
            z_wait(6, h, kind)
            go(z_copy(5, h, kind, 6, -1))
            if kind == V:
                go(z_copy(4, h, kind, 6, -2))

        @pl.when((y == 0) & (z > 0))
        def _(h=h):
            hand_over(1, h)

        @pl.when((y == YN - 1) & (z < ZN - 1))
        def _(h=h):
            hand_over(3, h)


    for k in range(1, YN):
        q_copy(FAR, k, YN).wait_recv()
    for h in range(HEADS):
        far(h, (0, 1, 7, 2, 6), first=True)
    for h in range(HEADS):
        for slot in (2, 4):
            for kind in (K, V):
                @pl.when(frame != (0 if slot == 2 else FRAMES - 1))
                def _(h=h, kind=kind, slot=slot):
                    n_wait(slot, h, kind)
                    n_copy(slot, h, kind, kn.at[slot - 1], vn.at[slot - 1], dc=1).wait_send()

        near(h, [(kn.at[1], vn.at[1], ZN), (kn.at[2], vn.at[2], ZN + 1), (kn.at[3], vn.at[3], ZN + 4), (kn.at[4], vn.at[4], ZN + 5)])
        send_out(NEAR, h, XN)
    for h in range(HEADS):
        for slot in (3, 5, 4):
            z_wait(slot, h, K)

        def values_wait(h=h):
            for slot in (3, 5, 4):
                z_wait(slot, h, V)

        far(h, (3, 5, 4), before_values=values_wait)
        send_out(FAR, h, YN)

    def merged(h, state, part):
        for k in range(3):
            for copy in o_copies(part, k + 1, 4, h):
                copy.wait_recv()
        high, count, out = state
        tops = [high] + [st_recv[part, k, h, 0:1] for k in range(3)]
        counts = [count] + [st_recv[part, k, h, 1:2] for k in range(3)]
        outs = [out] + [o_recv[part, k, h].astype(jnp.float32) for k in range(3)]
        new = functools.reduce(jnp.maximum, tops)
        factors = [jnp.exp2((t - new) * EXP2_SCALE) for t in tops]
        count = functools.reduce(jnp.add, [n * f for n, f in zip(counts, factors)])
        out = functools.reduce(jnp.add, [o * f for o, f in zip(outs, factors)])
        return new, count, out

    own = slice(0, ROWS)
    states = []
    for h in range(HEADS):
        one = (top[NEAR, h, :, own], total[NEAR, h, :, own], acc[NEAR, h, :, own])
        two = (top[FAR, h, :, own], total[FAR, h, :, own], acc[FAR, h, :, own])
        new = jnp.maximum(one[0], two[0])
        f1 = jnp.exp2((one[0] - new) * EXP2_SCALE)
        f2 = jnp.exp2((two[0] - new) * EXP2_SCALE)
        states.append(merged(h, (new, one[1] * f1 + two[1] * f2, one[2] * f1 + two[2] * f2), NEAR))
    for h in range(HEADS):
        _, count, out = merged(h, states[h], FAR)
        o_ref[:, h * HD:(h + 1) * HD] = (out / count).T.astype(jnp.bfloat16)
    for copy in started:
        copy.wait_send()

    @pl.when((y < YN - 1) | (z > 0))
    def _():
        for copy in before:
            copy.wait_send()

    @pl.when((y > 0) | (z < ZN - 1))
    def _():
        for copy in after:
            copy.wait_send()


def shards(queries, keys, values, band):
    vmem = pl.BlockSpec(memory_space=pltpu.VMEM)
    bf16, f32 = jnp.bfloat16, jnp.float32
    dma = pltpu.SemaphoreType.DMA
    width = HEADS * HD
    out = pl.pallas_call(
        kernel,
        out_shape=jax.ShapeDtypeStruct((ROWS, width), bf16),
        in_specs=[pl.BlockSpec(memory_space=pltpu.HBM)] * 4,
        out_specs=vmem,
        scratch_shapes=[
            pltpu.VMEM((ROWS, width), bf16),
            pltpu.VMEM((ROWS, width), bf16),
            pltpu.SMEM((FRAMES, FRAMES), jnp.int32),
            pltpu.VMEM((ZN, ROWS, width), bf16),
            pltpu.VMEM((ZN, width, ROWS), bf16),
            pltpu.VMEM((5, ROWS, width), bf16),
            pltpu.VMEM((5, width, ROWS), bf16),
            pltpu.VMEM((width, ROWS), bf16),
            pltpu.VMEM((2, 3, width, ROWS), bf16),
            pltpu.VMEM((ZN + 6, 1, 4 * ROWS), f32),
            pltpu.VMEM((2, HEADS, HD, 4 * ROWS), f32),
            pltpu.VMEM((2, HEADS, 1, 4 * ROWS), f32),
            pltpu.VMEM((2, HEADS, 1, 4 * ROWS), f32),
            pltpu.VMEM((2, 3, HEADS, HD, ROWS), bf16),
            pltpu.VMEM((2, 3, HEADS, 8, ROWS), f32),
            pltpu.VMEM((2, 3, HEADS, HD, ROWS), bf16),
            pltpu.VMEM((2, 3, HEADS, 8, ROWS), f32),
            dma((4,)),
            dma((ZN, HEADS, 2)), dma((ZN, HEADS, 2)),
            dma((5, HEADS, 2)), dma((5, HEADS, 2)),
            dma((2, 3)), dma((2, 3)),
            dma((2, 3, HEADS)), dma((2, 3, HEADS)),
            dma((2, 3, HEADS)), dma((2, 3, HEADS)),
        ],
        compiler_params=pltpu.CompilerParams(collective_id=0, has_side_effects=True, vmem_limit_bytes=55100 * 2 ** 10),
    )(queries[0], keys[0], values[0], band)
    return out[None]


def solution(mesh):
    spec = P("frame", "tok", None)
    return jax.shard_map(shards, mesh=mesh, in_specs=(spec, spec, spec, P()), out_specs=spec, check_vma=False)
```

```python
import functools
import math

import jax
import jax.numpy as jnp
from jax import lax
from jax.experimental import pallas as pl
from jax.experimental.pallas import tpu as pltpu
from jax.sharding import PartitionSpec as P

HEADS = 2
HD = 128
ROWS = 128
ZN, YN, XN, CN = 8, 4, 4, 2
FRAMES = ZN * YN
FAR, NEAR = 0, 1
K, V = 0, 1
HIDE = -1e30
LOW = -1e29
EXP2_SCALE = HD ** -0.5 * math.log2(math.e)


def coords():
    frame = lax.axis_index("frame")
    tok = lax.axis_index("tok")
    return lax.div(frame, YN), lax.rem(frame, YN), lax.div(tok, CN), lax.rem(tok, CN)


def kernel(
    q_ref, k_ref, v_ref, band_ref, o_ref,
    v_in, q_in, band_in, kz, vz, kn, vn, q_own, q_set, bias, acc, top, total,
    o_send, st_send, o_recv, st_recv,
    in_sem, z_ss, z_rs, n_ss, n_rs, q_ss, q_rs, o_ss, o_rs, s_ss, s_rs,
):
    z, y, x, c = coords()

    def at(dz=0, dy=0, dx=0, dc=0):
        frame = lax.rem(z + (dz + ZN), ZN) * YN + lax.rem(y + (dy + YN), YN)
        tok = lax.rem(x + (dx + XN), XN) * CN + lax.rem(c + dc, CN)
        return (frame, tok)

    def remote(src, dst, ss, rs, to):
        return pltpu.make_async_remote_copy(
            src_ref=src, dst_ref=dst, send_sem=ss, recv_sem=rs,
            device_id=to, device_id_type=pl.DeviceIdType.MESH,
        )

    barrier = pltpu.get_barrier_semaphore()
    peers = [at(dz=1), at(dz=-1), at(dz=2), at(dz=-2), at(dy=1), at(dy=2), at(dy=3), at(dx=1), at(dx=2), at(dx=3), at(dc=1)]
    for peer in peers:
        pl.semaphore_signal(barrier, inc=1, device_id=peer, device_id_type=pl.DeviceIdType.MESH)

    loads = [
        pltpu.make_async_copy(src, dst, in_sem.at[i])
        for i, (src, dst) in enumerate(((v_ref, v_in), (k_ref, kz.at[0]), (q_ref, q_in), (band_ref, band_in)))
    ]
    for load in loads:
        load.start()

    started = []

    def go(copy):
        copy.start()
        started.append(copy)

    def piece(keys, values, h, kind):
        part = pl.ds(h * HD, HD)
        return keys.at[:, part] if kind == K else values.at[part]

    def z_copy(slot, h, kind, src, dz):
        return remote(
            piece(kz.at[src], vz.at[src], h, kind), piece(kz.at[slot], vz.at[slot], h, kind),
            z_ss.at[slot, h, kind], z_rs.at[slot, h, kind], at(dz=dz),
        )

    def z_wait(slot, h, kind):
        z_copy(slot, h, kind, 0, 1).wait_recv()

    def n_copy(slot, h, kind, keys, values, **to):
        return remote(
            piece(keys, values, h, kind), piece(kn.at[slot], vn.at[slot], h, kind),
            n_ss.at[slot, h, kind], n_rs.at[slot, h, kind], at(**to),
        )

    def n_wait(slot, h, kind):
        n_copy(slot, h, kind, kz.at[0], vz.at[0], dc=1).wait_recv()

    def q_copy(part, k, n):
        to = at(dy=k) if part == FAR else at(dx=k)
        return remote(q_own, q_set.at[part, n - k - 1], q_ss.at[part, n - k - 1], q_rs.at[part, n - k - 1], to)

    def o_copies(part, k, n, h):
        to = at(dy=k) if part == FAR else at(dx=k)
        there = n - k - 1
        return (
            remote(o_send.at[part, k - 1, h], o_recv.at[part, there, h], o_ss.at[part, there, h], o_rs.at[part, there, h], to),
            remote(st_send.at[part, k - 1, h], st_recv.at[part, there, h], s_ss.at[part, there, h], s_rs.at[part, there, h], to),
        )

    frame = z * YN + y
    loads[0].wait()
    vz[0] = v_in[...].T
    loads[1].wait()
    pl.semaphore_wait(barrier, len(peers))

    for kind in (K, V):
        for h in range(HEADS):
            go(z_copy(1, h, kind, 0, 1))
            go(z_copy(7, h, kind, 0, -1))

    pieces = [(h, kind) for h in range(HEADS) for kind in (K, V)]
    before = [n_copy(1, h, kind, kz.at[0], vz.at[0], dy=1) for h, kind in pieces]
    after = [n_copy(3, h, kind, kz.at[0], vz.at[0], dy=-1) for h, kind in pieces]

    @pl.when((y < YN - 1))
    def _():
        for copy in before:
            copy.start()

    @pl.when(y > 0)
    def _():
        for copy in after:
            copy.start()

    for h, kind in pieces:
        go(n_copy(0, h, kind, kz.at[0], vz.at[0], dc=1))

    @pl.when(frame == 0)
    def _():
        kn[1:3] = jnp.zeros((2,) + kn.shape[1:], kn.dtype)
        vn[1:3] = jnp.zeros((2,) + vn.shape[1:], vn.dtype)

    @pl.when(frame == FRAMES - 1)
    def _():
        kn[3:5] = jnp.zeros((2,) + kn.shape[1:], kn.dtype)
        vn[3:5] = jnp.zeros((2,) + vn.shape[1:], vn.dtype)

    loads[2].wait()
    q_own[...] = q_in[...].T
    for k in (2, 1, 3):
        go(q_copy(NEAR, k, XN))
        go(q_copy(FAR, k, YN))
    loads[3].wait()
    lane = lax.broadcasted_iota(jnp.int32, (1, 4 * ROWS), 1) // ROWS

    def row_of(cells):
        row = jnp.full((1, 4 * ROWS), cells[0], jnp.float32)
        for k in range(1, 4):
            row = jnp.where(lane == k, cells[k], row)
        return row

    for slot in range(ZN):
        key_frame = lax.rem(z + (ZN - slot), ZN) * YN + y
        cells = []
        for k in range(YN):
            query_frame = z * YN + lax.rem(y + k, YN)
            seen = (jnp.abs(query_frame - key_frame) >= 2) & (band_in[query_frame, key_frame] >= 0)
            cells.append(jnp.where(seen, 0.0, HIDE).astype(jnp.float32))
        bias[slot] = row_of(cells)
    for step in range(3):
        key_frame = frame + (step - 1)
        inside = (key_frame >= 0) & (key_frame < FRAMES)
        reach = band_in[frame, jnp.clip(key_frame, 0, FRAMES - 1)]
        for other in range(CN):
            key_block = x * CN + lax.rem(c + other, CN)
            cells = []
            for k in range(XN):
                query_block = lax.rem(x + k, XN) * CN + c
                seen = inside & (jnp.abs(query_block - key_block) <= reach)
                cells.append(jnp.where(seen, 0.0, HIDE).astype(jnp.float32))
            bias[ZN + step * CN + other] = row_of(cells)

    def update(part, h, blocks, first, before_values=lambda: None):
        cols = pl.ds(h * HD, HD)
        qt = jnp.concatenate([q_own[cols]] + [q_set[part, k, cols] for k in range(3)], axis=1)
        rows = [bias[b] for _, _, b in blocks]
        scores = [jnp.dot(keys[:, cols], qt, preferred_element_type=jnp.float32) for keys, _, _ in blocks]
        high = functools.reduce(jnp.maximum, [jnp.max(s, axis=0, keepdims=True) + r for s, r in zip(scores, rows)])
        old = jnp.full((1, 4 * ROWS), LOW, jnp.float32) if first else top[part, h]
        new = jnp.maximum(old, high)
        weights = [jnp.exp2((s - (new - r)) * EXP2_SCALE) for s, r in zip(scores, rows)]
        add = functools.reduce(jnp.add, [jnp.sum(w, axis=0, keepdims=True) for w in weights])
        top[part, h] = new
        if first:
            total[part, h] = add
        else:
            factor = jnp.exp2((old - new) * EXP2_SCALE)
            total[part, h] = total[part, h] * factor + add
        wt = jnp.concatenate([w.astype(jnp.bfloat16) for w in weights], axis=0)
        before_values()
        vt = jnp.concatenate([values[cols] for _, values, _ in blocks], axis=1)
        out = jnp.dot(vt, wt, preferred_element_type=jnp.float32)
        if first:
            acc[part, h] = out
        else:
            acc[part, h] = acc[part, h] * factor + out

    def far(h, slots, first=False, before_values=lambda: None):
        update(FAR, h, [(kz.at[s], vz.at[s], s) for s in slots], first, before_values)

    def near(h, refs, first=False):
        update(NEAR, h, [(keys, values, b) for keys, values, b in refs], first)

    def send_out(part, h, n):
        for k in (2, 1, 3):
            cols = slice(k * ROWS, (k + 1) * ROWS)
            o_send[part, k - 1, h] = acc[part, h, :, cols].astype(jnp.bfloat16)
            st_send[part, k - 1, h] = jnp.concatenate(
                [top[part, h, :, cols], total[part, h, :, cols], jnp.zeros((6, ROWS), jnp.float32)], axis=0
            )
            for copy in o_copies(part, k, n, h):
                go(copy)

    for kind in (K, V):
        for h in range(HEADS):
            z_wait(1, h, kind)
            go(z_copy(2, h, kind, 1, 1))

            @pl.when((y == YN - 1) & (z > 0))
            def _(h=h, kind=kind):
                n_copy(1, h, kind, kz.at[1], vz.at[1], dy=1).start()

            z_wait(7, h, kind)
            go(z_copy(6, h, kind, 7, -1))

            @pl.when((y == 0) & (z < ZN - 1))
            def _(h=h, kind=kind):
                n_copy(3, h, kind, kz.at[7], vz.at[7], dy=-1).start()

    def hand_over(slot, h):
        for kind in (K, V):
            n_wait(slot, h, kind)
            n_copy(slot + 1, h, kind, kn.at[slot], vn.at[slot], dc=1).start()

    @pl.when(y > 0)
    def _():
        for h in range(HEADS):
            hand_over(1, h)

    @pl.when(y < YN - 1)
    def _():
        for h in range(HEADS):
            hand_over(3, h)

    for h, kind in pieces:
        n_wait(0, h, kind)
    for k in range(1, XN):
        q_copy(NEAR, k, XN).wait_recv()
    for h in range(HEADS):
        near(h, [(kz.at[0], vz.at[0], ZN + 2), (kn.at[0], vn.at[0], ZN + 3)], first=True)

    for h in range(HEADS):
        for kind in (K, V):
            z_wait(2, h, kind)
            go(z_copy(3, h, kind, 2, 1))
            if kind == K:
                go(z_copy(4, h, kind, 2, 2))
            z_wait(6, h, kind)
            go(z_copy(5, h, kind, 6, -1))
            if kind == V:
                go(z_copy(4, h, kind, 6, -2))

        @pl.when((y == 0) & (z > 0))
        def _(h=h):
            hand_over(1, h)

        @pl.when((y == YN - 1) & (z < ZN - 1))
        def _(h=h):
            hand_over(3, h)


    for k in range(1, YN):
        q_copy(FAR, k, YN).wait_recv()
    for h in range(HEADS):
        far(h, (0, 1, 7, 2, 6), first=True)
    for h in range(HEADS):
        for slot in (2, 4):
            for kind in (K, V):
                @pl.when(frame != (0 if slot == 2 else FRAMES - 1))
                def _(h=h, kind=kind, slot=slot):
                    n_wait(slot, h, kind)
                    n_copy(slot, h, kind, kn.at[slot - 1], vn.at[slot - 1], dc=1).wait_send()

        near(h, [(kn.at[1], vn.at[1], ZN), (kn.at[2], vn.at[2], ZN + 1), (kn.at[3], vn.at[3], ZN + 4), (kn.at[4], vn.at[4], ZN + 5)])
        send_out(NEAR, h, XN)
    for h in range(HEADS):
        for slot in (3, 5, 4):
            z_wait(slot, h, K)

        def values_wait(h=h):
            for slot in (3, 5, 4):
                z_wait(slot, h, V)

        far(h, (3, 5, 4), before_values=values_wait)
        send_out(FAR, h, YN)

    def merged(h, state, part):
        for k in range(3):
            for copy in o_copies(part, k + 1, 4, h):
                copy.wait_recv()
        high, count, out = state
        tops = [high] + [st_recv[part, k, h, 0:1] for k in range(3)]
        counts = [count] + [st_recv[part, k, h, 1:2] for k in range(3)]
        outs = [out] + [o_recv[part, k, h].astype(jnp.float32) for k in range(3)]
        new = functools.reduce(jnp.maximum, tops)
        factors = [jnp.exp2((t - new) * EXP2_SCALE) for t in tops]
        count = functools.reduce(jnp.add, [n * f for n, f in zip(counts, factors)])
        out = functools.reduce(jnp.add, [o * f for o, f in zip(outs, factors)])
        return new, count, out

    own = slice(0, ROWS)
    states = []
    for h in range(HEADS):
        one = (top[NEAR, h, :, own], total[NEAR, h, :, own], acc[NEAR, h, :, own])
        two = (top[FAR, h, :, own], total[FAR, h, :, own], acc[FAR, h, :, own])
        new = jnp.maximum(one[0], two[0])
        f1 = jnp.exp2((one[0] - new) * EXP2_SCALE)
        f2 = jnp.exp2((two[0] - new) * EXP2_SCALE)
        states.append(merged(h, (new, one[1] * f1 + two[1] * f2, one[2] * f1 + two[2] * f2), NEAR))
    for copy in started:
        copy.wait_send()

    @pl.when((y < YN - 1) | (z > 0))
    def _():
        for copy in before:
            copy.wait_send()

    @pl.when((y > 0) | (z < ZN - 1))
    def _():
        for copy in after:
            copy.wait_send()

    for h in range(HEADS):
        _, count, out = merged(h, states[h], FAR)
        o_ref[:, h * HD:(h + 1) * HD] = (out / count).T.astype(jnp.bfloat16)


def shards(queries, keys, values, band):
    vmem = pl.BlockSpec(memory_space=pltpu.VMEM)
    bf16, f32 = jnp.bfloat16, jnp.float32
    dma = pltpu.SemaphoreType.DMA
    width = HEADS * HD
    out = pl.pallas_call(
        kernel,
        out_shape=jax.ShapeDtypeStruct((ROWS, width), bf16),
        in_specs=[pl.BlockSpec(memory_space=pltpu.HBM)] * 4,
        out_specs=vmem,
        scratch_shapes=[
            pltpu.VMEM((ROWS, width), bf16),
            pltpu.VMEM((ROWS, width), bf16),
            pltpu.SMEM((FRAMES, FRAMES), jnp.int32),
            pltpu.VMEM((ZN, ROWS, width), bf16),
            pltpu.VMEM((ZN, width, ROWS), bf16),
            pltpu.VMEM((5, ROWS, width), bf16),
            pltpu.VMEM((5, width, ROWS), bf16),
            pltpu.VMEM((width, ROWS), bf16),
            pltpu.VMEM((2, 3, width, ROWS), bf16),
            pltpu.VMEM((ZN + 6, 1, 4 * ROWS), f32),
            pltpu.VMEM((2, HEADS, HD, 4 * ROWS), f32),
            pltpu.VMEM((2, HEADS, 1, 4 * ROWS), f32),
            pltpu.VMEM((2, HEADS, 1, 4 * ROWS), f32),
            pltpu.VMEM((2, 3, HEADS, HD, ROWS), bf16),
            pltpu.VMEM((2, 3, HEADS, 8, ROWS), f32),
            pltpu.VMEM((2, 3, HEADS, HD, ROWS), bf16),
            pltpu.VMEM((2, 3, HEADS, 8, ROWS), f32),
            dma((4,)),
            dma((ZN, HEADS, 2)), dma((ZN, HEADS, 2)),
            dma((5, HEADS, 2)), dma((5, HEADS, 2)),
            dma((2, 3)), dma((2, 3)),
            dma((2, 3, HEADS)), dma((2, 3, HEADS)),
            dma((2, 3, HEADS)), dma((2, 3, HEADS)),
        ],
        compiler_params=pltpu.CompilerParams(collective_id=0, has_side_effects=True, vmem_limit_bytes=55100 * 2 ** 10),
    )(queries[0], keys[0], values[0], band)
    return out[None]


def solution(mesh):
    spec = P("frame", "tok", None)
    return jax.shard_map(shards, mesh=mesh, in_specs=(spec, spec, spec, P()), out_specs=spec, check_vma=False)
```

```python
import functools
import math

import jax
import jax.numpy as jnp
from jax import lax
from jax.experimental import pallas as pl
from jax.experimental.pallas import tpu as pltpu
from jax.sharding import PartitionSpec as P

HEADS = 2
HD = 128
ROWS = 128
ZN, YN, XN, CN = 8, 4, 4, 2
FRAMES = ZN * YN
FAR, NEAR = 0, 1
K, V = 0, 1
HIDE = -1e30
LOW = -1e29
EXP2_SCALE = HD ** -0.5 * math.log2(math.e)


def coords():
    frame = lax.axis_index("frame")
    tok = lax.axis_index("tok")
    return lax.div(frame, YN), lax.rem(frame, YN), lax.div(tok, CN), lax.rem(tok, CN)


def kernel(
    q_ref, k_ref, v_ref, band_ref, o_ref,
    v_in, q_in, band_in, kz, vz, kn, vn, q_own, q_set, bias, acc, top, total,
    o_send, st_send, o_recv, st_recv,
    in_sem, z_ss, z_rs, n_ss, n_rs, q_ss, q_rs, o_ss, o_rs, s_ss, s_rs,
):
    z, y, x, c = coords()

    def at(dz=0, dy=0, dx=0, dc=0):
        frame = lax.rem(z + (dz + ZN), ZN) * YN + lax.rem(y + (dy + YN), YN)
        tok = lax.rem(x + (dx + XN), XN) * CN + lax.rem(c + dc, CN)
        return (frame, tok)

    def remote(src, dst, ss, rs, to):
        return pltpu.make_async_remote_copy(
            src_ref=src, dst_ref=dst, send_sem=ss, recv_sem=rs,
            device_id=to, device_id_type=pl.DeviceIdType.MESH,
        )

    barrier = pltpu.get_barrier_semaphore()
    peers = [at(dz=1), at(dz=-1), at(dz=2), at(dz=-2), at(dy=1), at(dy=2), at(dy=3), at(dx=1), at(dx=2), at(dx=3), at(dc=1)]
    for peer in peers:
        pl.semaphore_signal(barrier, inc=1, device_id=peer, device_id_type=pl.DeviceIdType.MESH)

    loads = [
        pltpu.make_async_copy(src, dst, in_sem.at[i])
        for i, (src, dst) in enumerate(((v_ref, v_in), (k_ref, kz.at[0]), (q_ref, q_in), (band_ref, band_in)))
    ]
    for load in loads:
        load.start()

    started = []

    def go(copy):
        copy.start()
        started.append(copy)

    def piece(keys, values, h, kind):
        part = pl.ds(h * HD, HD)
        return keys.at[:, part] if kind == K else values.at[part]

    def z_copy(slot, h, kind, src, dz):
        return remote(
            piece(kz.at[src], vz.at[src], h, kind), piece(kz.at[slot], vz.at[slot], h, kind),
            z_ss.at[slot, h, kind], z_rs.at[slot, h, kind], at(dz=dz),
        )

    def z_wait(slot, h, kind):
        z_copy(slot, h, kind, 0, 1).wait_recv()

    def n_copy(slot, h, kind, keys, values, **to):
        return remote(
            piece(keys, values, h, kind), piece(kn.at[slot], vn.at[slot], h, kind),
            n_ss.at[slot, h, kind], n_rs.at[slot, h, kind], at(**to),
        )

    def n_wait(slot, h, kind):
        n_copy(slot, h, kind, kz.at[0], vz.at[0], dc=1).wait_recv()

    def q_copy(part, k, n):
        to = at(dy=k) if part == FAR else at(dx=k)
        return remote(q_own, q_set.at[part, n - k - 1], q_ss.at[part, n - k - 1], q_rs.at[part, n - k - 1], to)

    def o_copies(part, k, n, h):
        to = at(dy=k) if part == FAR else at(dx=k)
        there = n - k - 1
        return (
            remote(o_send.at[part, k - 1, h], o_recv.at[part, there, h], o_ss.at[part, there, h], o_rs.at[part, there, h], to),
            remote(st_send.at[part, k - 1, h], st_recv.at[part, there, h], s_ss.at[part, there, h], s_rs.at[part, there, h], to),
        )

    frame = z * YN + y
    loads[0].wait()
    vz[0] = v_in[...].T
    loads[1].wait()
    pl.semaphore_wait(barrier, len(peers))

    for kind in (K, V):
        for h in range(HEADS):
            go(z_copy(1, h, kind, 0, 1))
            go(z_copy(7, h, kind, 0, -1))

    pieces = [(h, kind) for h in range(HEADS) for kind in (K, V)]
    before = [n_copy(1, h, kind, kz.at[0], vz.at[0], dy=1) for h, kind in pieces]
    after = [n_copy(3, h, kind, kz.at[0], vz.at[0], dy=-1) for h, kind in pieces]

    for one, other in zip(before, after):
        @pl.when(y < YN - 1)
        def _(one=one):
            one.start()

        @pl.when(y > 0)
        def _(other=other):
            other.start()

    for h, kind in pieces:
        go(n_copy(0, h, kind, kz.at[0], vz.at[0], dc=1))

    @pl.when(frame == 0)
    def _():
        kn[1:3] = jnp.zeros((2,) + kn.shape[1:], kn.dtype)
        vn[1:3] = jnp.zeros((2,) + vn.shape[1:], vn.dtype)

    @pl.when(frame == FRAMES - 1)
    def _():
        kn[3:5] = jnp.zeros((2,) + kn.shape[1:], kn.dtype)
        vn[3:5] = jnp.zeros((2,) + vn.shape[1:], vn.dtype)

    loads[2].wait()
    q_own[...] = q_in[...].T
    for k in (2, 1, 3):
        go(q_copy(NEAR, k, XN))
        go(q_copy(FAR, k, YN))
    loads[3].wait()
    lane = lax.broadcasted_iota(jnp.int32, (1, 4 * ROWS), 1) // ROWS

    def row_of(cells):
        row = jnp.full((1, 4 * ROWS), cells[0], jnp.float32)
        for k in range(1, 4):
            row = jnp.where(lane == k, cells[k], row)
        return row

    for slot in range(ZN):
        key_frame = lax.rem(z + (ZN - slot), ZN) * YN + y
        cells = []
        for k in range(YN):
            query_frame = z * YN + lax.rem(y + k, YN)
            seen = (jnp.abs(query_frame - key_frame) >= 2) & (band_in[query_frame, key_frame] >= 0)
            cells.append(jnp.where(seen, 0.0, HIDE).astype(jnp.float32))
        bias[slot] = row_of(cells)
    for step in range(3):
        key_frame = frame + (step - 1)
        inside = (key_frame >= 0) & (key_frame < FRAMES)
        reach = band_in[frame, jnp.clip(key_frame, 0, FRAMES - 1)]
        for other in range(CN):
            key_block = x * CN + lax.rem(c + other, CN)
            cells = []
            for k in range(XN):
                query_block = lax.rem(x + k, XN) * CN + c
                seen = inside & (jnp.abs(query_block - key_block) <= reach)
                cells.append(jnp.where(seen, 0.0, HIDE).astype(jnp.float32))
            bias[ZN + step * CN + other] = row_of(cells)

    def update(part, h, blocks, first, before_values=lambda: None):
        cols = pl.ds(h * HD, HD)
        qt = jnp.concatenate([q_own[cols]] + [q_set[part, k, cols] for k in range(3)], axis=1)
        rows = [bias[b] for _, _, b in blocks]
        scores = [jnp.dot(keys[:, cols], qt, preferred_element_type=jnp.float32) for keys, _, _ in blocks]
        high = functools.reduce(jnp.maximum, [jnp.max(s, axis=0, keepdims=True) + r for s, r in zip(scores, rows)])
        old = jnp.full((1, 4 * ROWS), LOW, jnp.float32) if first else top[part, h]
        new = jnp.maximum(old, high)
        weights = [jnp.exp2((s - (new - r)) * EXP2_SCALE) for s, r in zip(scores, rows)]
        add = functools.reduce(jnp.add, [jnp.sum(w, axis=0, keepdims=True) for w in weights])
        top[part, h] = new
        if first:
            total[part, h] = add
        else:
            factor = jnp.exp2((old - new) * EXP2_SCALE)
            total[part, h] = total[part, h] * factor + add
        wt = jnp.concatenate([w.astype(jnp.bfloat16) for w in weights], axis=0)
        before_values()
        vt = jnp.concatenate([values[cols] for _, values, _ in blocks], axis=1)
        out = jnp.dot(vt, wt, preferred_element_type=jnp.float32)
        if first:
            acc[part, h] = out
        else:
            acc[part, h] = acc[part, h] * factor + out

    def far(h, slots, first=False, before_values=lambda: None):
        update(FAR, h, [(kz.at[s], vz.at[s], s) for s in slots], first, before_values)

    def near(h, refs, first=False):
        update(NEAR, h, [(keys, values, b) for keys, values, b in refs], first)

    def send_out(part, h, n):
        for k in (2, 1, 3):
            cols = slice(k * ROWS, (k + 1) * ROWS)
            o_send[part, k - 1, h] = acc[part, h, :, cols].astype(jnp.bfloat16)
            st_send[part, k - 1, h] = jnp.concatenate(
                [top[part, h, :, cols], total[part, h, :, cols], jnp.zeros((6, ROWS), jnp.float32)], axis=0
            )
            for copy in o_copies(part, k, n, h):
                go(copy)

    for kind in (K, V):
        for h in range(HEADS):
            z_wait(1, h, kind)
            go(z_copy(2, h, kind, 1, 1))

            @pl.when((y == YN - 1) & (z > 0))
            def _(h=h, kind=kind):
                n_copy(1, h, kind, kz.at[1], vz.at[1], dy=1).start()

            z_wait(7, h, kind)
            go(z_copy(6, h, kind, 7, -1))

            @pl.when((y == 0) & (z < ZN - 1))
            def _(h=h, kind=kind):
                n_copy(3, h, kind, kz.at[7], vz.at[7], dy=-1).start()

    def hand_over(slot, h, kinds=(K, V)):
        for kind in kinds:
            n_wait(slot, h, kind)
            n_copy(slot + 1, h, kind, kn.at[slot], vn.at[slot], dc=1).start()

    @pl.when(y > 0)
    def _():
        for h in range(HEADS):
            hand_over(1, h)

    @pl.when(y < YN - 1)
    def _():
        for h in range(HEADS):
            hand_over(3, h)

    for h, kind in pieces:
        n_wait(0, h, kind)
    for k in range(1, XN):
        q_copy(NEAR, k, XN).wait_recv()
    for h in range(HEADS):
        near(h, [(kz.at[0], vz.at[0], ZN + 2), (kn.at[0], vn.at[0], ZN + 3)], first=True)

    for h in range(HEADS):
        for kind in (K, V):
            z_wait(2, h, kind)
            if kind == K:
                go(z_copy(4, h, kind, 2, 2))
            go(z_copy(3, h, kind, 2, 1))
            z_wait(6, h, kind)
            if kind == V:
                go(z_copy(4, h, kind, 6, -2))
            go(z_copy(5, h, kind, 6, -1))

            @pl.when((y == 0) & (z > 0))
            def _(h=h, kind=kind):
                hand_over(1, h, (kind,))

            @pl.when((y == YN - 1) & (z < ZN - 1))
            def _(h=h, kind=kind):
                hand_over(3, h, (kind,))


    for k in range(1, YN):
        q_copy(FAR, k, YN).wait_recv()
    for h in range(HEADS):
        far(h, (0, 1, 7, 2, 6), first=True)
    for h in range(HEADS):
        for slot in (2, 4):
            for kind in (K, V):
                @pl.when(frame != (0 if slot == 2 else FRAMES - 1))
                def _(h=h, kind=kind, slot=slot):
                    n_wait(slot, h, kind)
                    n_copy(slot, h, kind, kn.at[slot - 1], vn.at[slot - 1], dc=1).wait_send()

        near(h, [(kn.at[1], vn.at[1], ZN), (kn.at[2], vn.at[2], ZN + 1), (kn.at[3], vn.at[3], ZN + 4), (kn.at[4], vn.at[4], ZN + 5)])
        send_out(NEAR, h, XN)
    for h in range(HEADS):
        for slot in (3, 5, 4):
            z_wait(slot, h, K)

        def values_wait(h=h):
            for slot in (3, 5, 4):
                z_wait(slot, h, V)

        far(h, (3, 5, 4), before_values=values_wait)
        send_out(FAR, h, YN)

    def merged(h, state, part):
        for k in range(3):
            for copy in o_copies(part, k + 1, 4, h):
                copy.wait_recv()
        high, count, out = state
        tops = [high] + [st_recv[part, k, h, 0:1] for k in range(3)]
        counts = [count] + [st_recv[part, k, h, 1:2] for k in range(3)]
        outs = [out] + [o_recv[part, k, h].astype(jnp.float32) for k in range(3)]
        new = functools.reduce(jnp.maximum, tops)
        factors = [jnp.exp2((t - new) * EXP2_SCALE) for t in tops]
        count = functools.reduce(jnp.add, [n * f for n, f in zip(counts, factors)])
        out = functools.reduce(jnp.add, [o * f for o, f in zip(outs, factors)])
        return new, count, out

    own = slice(0, ROWS)
    states = []
    for h in range(HEADS):
        one = (top[NEAR, h, :, own], total[NEAR, h, :, own], acc[NEAR, h, :, own])
        two = (top[FAR, h, :, own], total[FAR, h, :, own], acc[FAR, h, :, own])
        new = jnp.maximum(one[0], two[0])
        f1 = jnp.exp2((one[0] - new) * EXP2_SCALE)
        f2 = jnp.exp2((two[0] - new) * EXP2_SCALE)
        states.append(merged(h, (new, one[1] * f1 + two[1] * f2, one[2] * f1 + two[2] * f2), NEAR))
    for copy in started:
        copy.wait_send()

    @pl.when((y < YN - 1) | (z > 0))
    def _():
        for copy in before:
            copy.wait_send()

    @pl.when((y > 0) | (z < ZN - 1))
    def _():
        for copy in after:
            copy.wait_send()

    for h in range(HEADS):
        _, count, out = merged(h, states[h], FAR)
        o_ref[:, h * HD:(h + 1) * HD] = (out / count).T.astype(jnp.bfloat16)


def shards(queries, keys, values, band):
    vmem = pl.BlockSpec(memory_space=pltpu.VMEM)
    bf16, f32 = jnp.bfloat16, jnp.float32
    dma = pltpu.SemaphoreType.DMA
    width = HEADS * HD
    out = pl.pallas_call(
        kernel,
        out_shape=jax.ShapeDtypeStruct((ROWS, width), bf16),
        in_specs=[pl.BlockSpec(memory_space=pltpu.HBM)] * 4,
        out_specs=vmem,
        scratch_shapes=[
            pltpu.VMEM((ROWS, width), bf16),
            pltpu.VMEM((ROWS, width), bf16),
            pltpu.SMEM((FRAMES, FRAMES), jnp.int32),
            pltpu.VMEM((ZN, ROWS, width), bf16),
            pltpu.VMEM((ZN, width, ROWS), bf16),
            pltpu.VMEM((5, ROWS, width), bf16),
            pltpu.VMEM((5, width, ROWS), bf16),
            pltpu.VMEM((width, ROWS), bf16),
            pltpu.VMEM((2, 3, width, ROWS), bf16),
            pltpu.VMEM((ZN + 6, 1, 4 * ROWS), f32),
            pltpu.VMEM((2, HEADS, HD, 4 * ROWS), f32),
            pltpu.VMEM((2, HEADS, 1, 4 * ROWS), f32),
            pltpu.VMEM((2, HEADS, 1, 4 * ROWS), f32),
            pltpu.VMEM((2, 3, HEADS, HD, ROWS), bf16),
            pltpu.VMEM((2, 3, HEADS, 8, ROWS), f32),
            pltpu.VMEM((2, 3, HEADS, HD, ROWS), bf16),
            pltpu.VMEM((2, 3, HEADS, 8, ROWS), f32),
            dma((4,)),
            dma((ZN, HEADS, 2)), dma((ZN, HEADS, 2)),
            dma((5, HEADS, 2)), dma((5, HEADS, 2)),
            dma((2, 3)), dma((2, 3)),
            dma((2, 3, HEADS)), dma((2, 3, HEADS)),
            dma((2, 3, HEADS)), dma((2, 3, HEADS)),
        ],
        compiler_params=pltpu.CompilerParams(collective_id=0, has_side_effects=True, vmem_limit_bytes=55100 * 2 ** 10),
    )(queries[0], keys[0], values[0], band)
    return out[None]


def solution(mesh):
    spec = P("frame", "tok", None)
    return jax.shard_map(shards, mesh=mesh, in_specs=(spec, spec, spec, P()), out_specs=spec, check_vma=False)
```
